256 devices in a mesh: section: 16 (over x, z_lo, core), seq: 16 (over y, z_hi).
Axes of the slice: x: 4, y: 4, z: 8 (z_hi: 4, z_lo: 2; z = z_hi * 2 + z_lo), core: 2. Of those that a mesh axis runs over, the one named last changes fastest.
Arguments:
- embed_table: bfloat16 [131072, 5376], P(('section', 'seq')), may hold values from -72 to 72
- vocab_shard: int32 [2048, 1], P('seq'), may hold values from 0 to 255; in each aligned block of 128 rows (0 to 127, 128 to 255, ...) at most 2 rows name the same one
- shard_row: int32 [2048], P('seq'), may hold values from 0 to 511
- norm_gain: bfloat16 [5376], replicated, may hold values from 0.099609375 to 1.8984375
- weight: bfloat16 [5376, 8192], P('seq', 'section'), may hold values from -0.078125 to 0.078125
- cotangent: bfloat16 [2048, 8192], P('seq', 'section'), may hold values from -6 to 6
Outputs:
- projected: bfloat16 [2048, 8192], P('seq', 'section')
- table_grad: bfloat16 [131072, 5376], P(('section', 'seq'))
- weight_grad: bfloat16 [5376, 8192], P('seq', 'section')
The draws below stay inside these ranges and needn't reach their ends.
Inputs may be any that keep to these rules, and one draw needn't show every extreme that they name: `vocab_shard`: in each aligned block of 128 tokens no shard is named by more than 2 tokens, a bound that some block reaches.
All inputs are finite; a program needn't handle non-finite values.
Results may differ from the reference program's by a relative error of at most 0.024.
Values may be sent and summed in bfloat16 or wider, within the bound.
No kernel may reach another device: no remote copies, remote signals or barrier semaphores. Data moves between devices by JAX's collectives and lax.ppermute only.
A program may use at most 128 MiB of HBM per device.

```python
import math
import jax
import jax.numpy as jnp
import numpy as np
from jax import lax

D = 5376
VROWS_DEV = 512
TOK_DEV = 128
TOKENS = 2048
VOCAB = 131072
QKV = 8192
CAP = 2
N_SECTION = 16
N_SEQ = 16


def draw_embed_table(key, part):
    key = jax.random.fold_in(key, 7)
    key_base, key_row, key_col = jax.random.split(key, 3)
    base = jnp.clip(jax.random.normal(key_base, (VOCAB, D), jnp.float32), -6.0, 6.0)
    row_scale = jnp.exp(jax.random.uniform(key_row, (VOCAB, 1), jnp.float32, 0.0, math.log(10.0)))
    col_scale = jnp.exp(jax.random.uniform(key_col, (1, D), jnp.float32, 0.0, math.log(4.0)))
    return (0.3 * base * row_scale * col_scale).astype(jnp.bfloat16)


def place_ends(result, stream_key, least, high):
    dims = result.shape
    index_at = [jax.random.randint(jax.random.fold_in(stream_key, axis), (), 0, dims[axis]) for axis in range(len(dims))]
    result = result.at[tuple(index_at)].set(least)
    longest = dims.index(max(dims))
    index_at[longest] = (index_at[longest] + 1) % dims[longest]
    return result.at[tuple(index_at)].set(high)


def shard_levels(own_key, dims, cuts, smallest, high):
    def one(position, parts):
        heights = jax.random.uniform(jax.random.fold_in(jax.random.fold_in(own_key, 6), position), (parts,), jnp.float32, smallest / len(cuts), high / len(cuts))
        return jnp.repeat(jnp.exp(heights), dims[position] // parts).reshape((-1,) + (1,) * (len(dims) - position - 1))

    level = one(*cuts[0])
    for cut in cuts[1:]:
        level = level * one(*cut)
    return level


def assign_block(key, own, number, rows, count, top, most, lean):
    ranking = jax.random.permutation(key, count)
    packed, ordinary = shares(count, rows * top, most, lean, True), shares(count, rows * top, most, lean, False)
    places = jnp.arange(count)

    def named(sizes, offset_by):
        used = int((sizes > 0).sum())
        fixed = max(1, used // 4)
        passed = fixed + (places - fixed + offset_by * (used - fixed)) % max(1, count - fixed)
        return jnp.zeros((count,), jnp.int32).at[ranking[jnp.where(places < fixed, places, passed)]].set(jnp.asarray(sizes, jnp.int32))

    sizes = jnp.where(number % 4 == 0, named(packed, number // 4), named(ordinary, number - number // 4 - 1))
    mixed = jax.random.permutation(jax.random.fold_in(own, 3), count)
    source_of, receiver = mixed[0:count // 2 * 2:2], mixed[1:count // 2 * 2:2]
    slack = jnp.minimum(sizes[source_of] - 1, most - sizes[receiver]) // 2
    slack = jnp.where((source_of == ranking[0]) | (receiver == ranking[0]) | (sizes[receiver] == 0), 0, jnp.maximum(slack, 0))
    passed = jax.random.randint(jax.random.fold_in(own, 4), (count // 2,), 0, 1 << 20) % (slack + 1)
    sizes = sizes.at[source_of].add(-passed).at[receiver].add(passed)
    labels = jnp.searchsorted(jnp.cumsum(sizes), jnp.arange(rows * top), side="right").astype(jnp.int32)
    grid = labels.reshape(top, rows).T
    grid = grid[jax.random.permutation(jax.random.fold_in(own, 1), rows)]
    offset_by = jax.random.randint(jax.random.fold_in(own, 2), (rows, 1), 0, top)
    return jnp.take_along_axis(grid, (jnp.arange(top)[None, :] + offset_by) % top, axis=1)


def shares(number_of, total, most, slope, full):
    loads = [(1 << 20) // math.isqrt(grade ** slope) + 1 for grade in range(1, number_of + 1)]
    largest = most if full else min(most, max(-(-total // number_of), total * loads[0] // sum(loads)))
    least = 1 if total - largest >= number_of - 1 else 0
    holding, surplus = [largest] + [least] * (number_of - 1), total - largest - least * (number_of - 1)
    while surplus > 0:
        candidates = [i for i in range(1, number_of) if holding[i] < largest] or [i for i in range(1, number_of) if holding[i] < most]
        mass, left = sum([loads[i] for i in candidates]), surplus
        for i in candidates:
            more = min(most - holding[i], max(1, left * loads[i] // mass), surplus)
            holding[i] = holding[i] + more
            surplus = surplus - more
    return np.array(holding)


def gaussian(own_key, shape, scale, limit, shards=(), kind=jnp.bfloat16):
    loudness = shard_levels(own_key, shape, shards, -0.22, 0.18) if shards else 1.0
    drawn = jax.random.normal(own_key, shape, jnp.float32) * scale * loudness
    return jnp.minimum(jnp.maximum(drawn, -limit), limit).astype(kind)


def setup_inputs(seed: int = 0) -> dict:
    key_list = jax.random.split(jax.random.key(seed), 7)
    embed_table = draw_embed_table(jax.random.fold_in(key_list[6], 71), 0)
    vocab_shard_keys = jax.random.split(jax.random.fold_in(key_list[1], 1), TOKENS // TOK_DEV)
    vocab_shard_turns = jax.random.permutation(jax.random.fold_in(key_list[1], 3), TOKENS // TOK_DEV)
    vocab_shard = jax.vmap(lambda own, number: assign_block(jax.random.fold_in(key_list[1], 2), own, number, TOK_DEV, N_SECTION * N_SEQ, 1, CAP, 1))(vocab_shard_keys, vocab_shard_turns).reshape((TOKENS, 1))
    shard_row = place_ends(jax.random.randint(key_list[2], (TOKENS,), 0, VROWS_DEV), jax.random.fold_in(key_list[2], 1), 0, VROWS_DEV - 1).astype(jnp.int32)
    norm_gain = jnp.clip(1.0 + 0.18 * jax.random.normal(key_list[3], (D,), jnp.float32), 0.099609375, 1.8984375).astype(jnp.bfloat16)
    weight = gaussian(key_list[4], (D, QKV), D ** -0.5, 0.078125, ((0, 16), (1, 16)))
    cotangent = gaussian(key_list[5], (TOKENS, QKV), 1.0, 6.0, ((0, 16), (1, 16)))
    return dict(embed_table=embed_table, vocab_shard=vocab_shard, shard_row=shard_row, norm_gain=norm_gain, weight=weight, cotangent=cotangent)


EPS = 1e-06

def reference(embed_table, vocab_shard, shard_row, norm_gain, weight, cotangent):
    token_ids = vocab_shard[:, 0] * VROWS_DEV + shard_row
    embedded = jnp.take(embed_table, token_ids, axis=0).astype(jnp.float32)
    inv_rms = lax.rsqrt(lax.optimization_barrier(jnp.mean(embedded * embedded, axis=-1, keepdims=True)) + EPS)
    unit_rows = embedded * inv_rms
    gain_full = norm_gain.astype(jnp.float32)
    normed = (unit_rows * gain_full).astype(jnp.bfloat16)
    projected = jnp.dot(normed, weight, preferred_element_type=jnp.float32).astype(jnp.bfloat16)
    upstream = lax.dot_general(cotangent, weight, (((1,), (1,)), ((), ())), preferred_element_type=jnp.float32)
    scaled = upstream * gain_full
    row_grads = (inv_rms * (scaled - unit_rows * lax.optimization_barrier(jnp.mean(scaled * unit_rows, axis=-1, keepdims=True)))).astype(jnp.bfloat16)
    grads_wide = lax.optimization_barrier(row_grads).astype(jnp.float32)
    owner_shard = vocab_shard[:, 0]

    def shard_grad(index):
        local_rows = jnp.where(owner_shard == index, shard_row, VROWS_DEV).astype(jnp.int32)
        summed = jax.ops.segment_sum(grads_wide, local_rows, num_segments=VROWS_DEV + 1)
        return summed[:VROWS_DEV].astype(jnp.bfloat16)
    table_grad = lax.map(shard_grad, jnp.arange(N_SECTION * N_SEQ, dtype=jnp.int32)).reshape(VOCAB, D)
    normed_blocks = normed.reshape(N_SEQ, TOK_DEV, D)
    cot_blocks = cotangent.reshape(N_SEQ, TOK_DEV, QKV)

    def add_block(total, pair):
        block_term = lax.dot_general(pair[0], pair[1], (((0,), (0,)), ((), ())), preferred_element_type=jnp.float32).astype(jnp.bfloat16)
        return (total + lax.optimization_barrier(block_term).astype(jnp.float32), None)
    total, unused = lax.scan(add_block, jnp.zeros((D, QKV), jnp.float32), (normed_blocks, cot_blocks))
    return (projected, table_grad, total.astype(jnp.bfloat16))
```

```python
import jax
import jax.numpy as jnp
from jax import lax
from jax.sharding import Mesh, PartitionSpec as P

EPS = 1e-06
SECTION = ("x", "z_lo", "core")
SEQ = ("y", "z_hi")
CAP = 2
BF16 = jnp.bfloat16
F32 = jnp.float32


def dot(a, b, contract):
    return lax.dot_general(a, b, (contract, ((), ())), preferred_element_type=F32)


def swap_cores(x):
    return lax.ppermute(x, "core", [(0, 1), (1, 0)])


def exchange(x, axes):
    return lax.all_to_all(x, axes, split_axis=0, concat_axis=0, tiled=True)


def owner_rows(token_ids, shard, vocab_rows):
    tokens = token_ids.shape[1]
    mine = token_ids // vocab_rows == shard
    place = jnp.arange(tokens, dtype=jnp.int32)[None, :]
    first = jnp.min(jnp.where(mine, place, tokens), axis=1, keepdims=True)
    last = jnp.max(jnp.where(mine, place, -1), axis=1, keepdims=True)
    row = token_ids % vocab_rows
    row_first = jnp.sum(jnp.where(place == first, row, 0), axis=1)
    row_last = jnp.sum(jnp.where(place == last, row, 0), axis=1)
    some = last[:, 0] >= 0
    two = jnp.logical_and(some, last[:, 0] != first[:, 0])
    return jnp.stack([jnp.where(some, row_first, -1), jnp.where(two, row_last, -1)], axis=1)


def token_slots(block_ids, vocab_rows):
    shard = block_ids // vocab_rows
    place = jnp.arange(shard.shape[0], dtype=jnp.int32)
    earlier = jnp.logical_and(shard[:, None] == shard[None, :], place[None, :] < place[:, None])
    return shard * CAP + jnp.sum(earlier.astype(jnp.int32), axis=1)


def per_device(embed_table, vocab_shard, shard_row, norm_gain, weight, cotangent):
    nx, nzl, nc = (lax.axis_size(a) for a in SECTION)
    ny, nzh = (lax.axis_size(a) for a in SEQ)
    n_section, n_seq = nx * nzl * nc, ny * nzh
    vocab_rows, model_width = embed_table.shape
    tok = shard_row.shape[0]
    feat, cols = weight.shape
    section, seq = lax.axis_index(SECTION), lax.axis_index(SEQ)
    core, y = lax.axis_index("core"), lax.axis_index("y")
    section_x = lax.axis_index("x")
    nb, nf = nx, nzl * nc
    block_slots = n_seq * CAP
    slots = n_section * block_slots

    ids = vocab_shard[:, 0] * vocab_rows + shard_row
    all_ids = exchange(jnp.broadcast_to(ids[None], (n_seq, tok)), SEQ)

    w_y = lax.all_gather(weight, "y", axis=0)
    cot = lax.all_gather(cotangent, "z_hi", axis=0, tiled=True)
    w_y = w_y.reshape(nzl, nc, feat, cols)
    w_own = lax.dynamic_index_in_dim(w_y, core, 1, keepdims=False)
    w_other = lax.dynamic_index_in_dim(w_y, 1 - core, 1, keepdims=False)

    wanted = owner_rows(all_ids, section * n_seq + seq, vocab_rows).reshape(-1)
    found = jnp.take(embed_table, jnp.maximum(wanted, 0), axis=0)
    embedded = jnp.where((wanted >= 0)[:, None], found, jnp.zeros((), BF16)).astype(F32)
    inv_rms = lax.rsqrt(jnp.mean(embedded * embedded, axis=-1, keepdims=True) + EPS)
    unit_rows = embedded * inv_rms
    gain_full = norm_gain.astype(F32)
    normed_rows = (unit_rows * gain_full).astype(BF16)

    out_rows = normed_rows.reshape(ny, nb * CAP, nf, nzh, feat).transpose(0, 3, 2, 1, 4)
    got = exchange(out_rows.reshape(n_seq, nf * nb * CAP, feat), SEQ)
    got = got.reshape(n_seq, nf, nb, CAP, feat).transpose(2, 1, 0, 3, 4)
    got = exchange(got.reshape(n_section, block_slots, feat), SECTION)
    block_ids = lax.dynamic_index_in_dim(all_ids, y * nzh + section_x, 0, keepdims=False)
    slot = token_slots(block_ids, vocab_rows)
    place = (slot[:, None] == jnp.arange(slots, dtype=jnp.int32)[None, :]).astype(BF16)
    normed_block = dot(place, got.reshape(slots, feat), ((1,), (0,))).astype(BF16)

    n_own = lax.all_gather(normed_block, ("x", "z_lo"), axis=0).reshape(nb, nzl, tok, feat)
    n_other = swap_cores(n_own)

    def partial_up(w):
        return jnp.stack([dot(cot, w[k], ((1,), (1,))) for k in range(nzl)])
    up = partial_up(w_own) + swap_cores(partial_up(w_other).astype(BF16)).astype(F32)
    up = up.astype(BF16).reshape(nzl, nb, tok, feat).transpose(1, 0, 2, 3)
    up = exchange(up.reshape(nb * nzl, tok, feat), ("x", "z_lo"))
    up = jnp.sum(up.astype(F32), axis=0).astype(BF16)
    back = dot(place, up, ((0,), (0,))).astype(BF16).reshape(n_section, block_slots, feat)
    back = exchange(back, SECTION).reshape(nb, nf, n_seq, CAP, feat).transpose(2, 1, 0, 3, 4)
    back = exchange(back.reshape(n_seq, nf * nb * CAP, feat), SEQ)
    back = back.reshape(ny, nzh, nf, nb * CAP, feat).transpose(0, 3, 2, 1, 4)
    upstream = back.reshape(n_seq * CAP, model_width).astype(F32)
    scaled = upstream * gain_full
    row_grads = (
        inv_rms * (scaled - unit_rows * jnp.mean(scaled * unit_rows, axis=-1, keepdims=True))
    ).astype(BF16)
    pick = (jnp.arange(vocab_rows, dtype=jnp.int32)[:, None] == wanted[None, :]).astype(BF16)
    table_grad = dot(pick, row_grads, ((1,), (0,))).astype(BF16)

    def tokens_of(n, k):
        return n[:, k].reshape(nb * tok, feat)
    proj = sum(
        dot(tokens_of(n, k), w[k], ((1,), (0,)))
        for n, w in ((n_own, w_own), (n_other, w_other)) for k in range(nzl)
    )
    proj = exchange(proj.astype(BF16).reshape(nzh, tok, cols), "z_hi")
    projected = jnp.sum(proj.astype(F32), axis=0).astype(BF16)

    g_own = jnp.stack([dot(tokens_of(n_own, k), cot, ((0,), (0,))).astype(BF16) for k in range(nzl)])
    g_other = jnp.stack([dot(tokens_of(n_other, k), cot, ((0,), (0,))).astype(BF16) for k in range(nzl)])
    first, second = jnp.where(core == 0, g_own, g_other), jnp.where(core == 0, g_other, g_own)
    grad = jnp.stack([first, second], axis=1).reshape(ny, feat, cols)
    grad = exchange(grad, "y")
    weight_grad = jnp.sum(grad.astype(F32), axis=0).astype(BF16)
    return projected, table_grad, weight_grad


def solution(mesh):
    devices = mesh.devices.reshape(4, 2, 2, 4, 4)
    fine = Mesh(devices, SECTION + SEQ)
    in_specs = (
        P(SECTION + SEQ, None),
        P(SEQ, None),
        P(SEQ),
        P(),
        P(SEQ, SECTION),
        P(SEQ, SECTION),
    )
    out_specs = (P(SEQ, SECTION), P(SECTION + SEQ, None), P(SEQ, SECTION))
    return jax.shard_map(
        per_device, mesh=fine, in_specs=in_specs, out_specs=out_specs, check_vma=False
    )
```

```python
import jax
import jax.numpy as jnp
from jax import lax
from jax.sharding import Mesh, PartitionSpec as P

EPS = 1e-06
SECTION = ("x", "z_lo", "core")
SEQ = ("y", "z_hi")
CAP = 2
BF16 = jnp.bfloat16
F32 = jnp.float32


def dot(a, b, contract):
    return lax.dot_general(a, b, (contract, ((), ())), preferred_element_type=F32)


def shift(x, axis, by):
    size = lax.axis_size(axis)
    return lax.ppermute(x, axis, [(i, (i + by) % size) for i in range(size)])


def exchange(x, axes):
    return lax.all_to_all(x, axes, split_axis=0, concat_axis=0, tiled=True)


def pick(x, index):
    return lax.dynamic_index_in_dim(x, index, 0, keepdims=False)


def sum_f32(parts):
    total = parts[0].astype(F32)
    for part in parts[1:]:
        total = total + part.astype(F32)
    return total


def owner_rows(token_ids, shard, vocab_rows):
    tokens = token_ids.shape[1]
    mine = token_ids // vocab_rows == shard
    place = jnp.arange(tokens, dtype=jnp.int32)[None, :]
    first = jnp.min(jnp.where(mine, place, tokens), axis=1, keepdims=True)
    last = jnp.max(jnp.where(mine, place, -1), axis=1, keepdims=True)
    row = token_ids % vocab_rows
    row_first = jnp.sum(jnp.where(place == first, row, 0), axis=1)
    row_last = jnp.sum(jnp.where(place == last, row, 0), axis=1)
    some = last[:, 0] >= 0
    two = jnp.logical_and(some, last[:, 0] != first[:, 0])
    return jnp.stack([jnp.where(some, row_first, -1), jnp.where(two, row_last, -1)], axis=1)


def token_slots(block_ids, vocab_rows):
    shard = block_ids // vocab_rows
    place = jnp.arange(shard.shape[0], dtype=jnp.int32)
    earlier = jnp.logical_and(shard[:, None] == shard[None, :], place[None, :] < place[:, None])
    return shard * CAP + jnp.sum(earlier.astype(jnp.int32), axis=1)


def per_device(embed_table, vocab_shard, shard_row, norm_gain, weight, cotangent):
    nx, nzl, nc = (lax.axis_size(a) for a in SECTION)
    ny, nzh = (lax.axis_size(a) for a in SEQ)
    n_section, n_seq = nx * nzl * nc, ny * nzh
    vocab_rows, model_width = embed_table.shape
    tok = shard_row.shape[0]
    feat, cols = weight.shape
    section, seq = lax.axis_index(SECTION), lax.axis_index(SEQ)
    ix, iz, ic, iy, ih = (lax.axis_index(a) for a in SECTION + SEQ)
    nb, nf = nx, nzl * nc
    block_slots = n_seq * CAP
    slots = n_section * block_slots

    ids = vocab_shard[:, 0] * vocab_rows + shard_row
    all_ids = exchange(jnp.broadcast_to(ids[None], (n_seq, tok)), SEQ)

    cot = [shift(cotangent, "z_hi", d) for d in range(nzh - 1, 0, -1)] + [cotangent]
    cot, all_ids = lax.optimization_barrier((jnp.stack(cot + cot), all_ids))
    cot = lax.dynamic_slice_in_dim(cot, (ix - ih) % nx, nx, 0)[::-1]
    cot = cot.reshape(nx * tok, cols)

    w = jnp.stack([weight] + [shift(weight, "y", d) for d in range(1, ny)])
    w = [
        jnp.concatenate([pick(w, (iy - (iz ^ z) * nc - (ic ^ c)) % ny) for z in range(nzl)], axis=0)
        for c in range(nc)
    ]

    wanted = owner_rows(all_ids, section * n_seq + seq, vocab_rows).reshape(-1)
    pick_matrix = (jnp.arange(vocab_rows, dtype=jnp.int32)[:, None] == wanted[None, :]).astype(BF16)
    embedded = dot(pick_matrix, embed_table, ((0,), (0,)))
    inv_rms = lax.rsqrt(jnp.mean(embedded * embedded, axis=-1, keepdims=True) + EPS)
    unit_rows = embedded * inv_rms
    gain_full = norm_gain.astype(F32)
    normed_rows = (unit_rows * gain_full).astype(BF16)

    out_rows = normed_rows.reshape(ny, nb * CAP, nf, nzh, feat).transpose(0, 3, 2, 1, 4)
    got = exchange(out_rows.reshape(n_seq, nf * nb * CAP, feat), SEQ)
    got = got.reshape(n_seq, nf, nb, CAP, feat).transpose(2, 1, 0, 3, 4)
    got = exchange(got.reshape(n_section, block_slots, feat), SECTION)
    block_ids = pick(all_ids, iy * nzh + ix)
    slot = token_slots(block_ids, vocab_rows)
    place = (jnp.arange(slots, dtype=jnp.int32)[:, None] == slot[None, :]).astype(BF16)
    normed = dot(got.reshape(slots, feat), place, ((0,), (0,))).astype(BF16)

    normed = jnp.concatenate([normed, shift(normed, "z_lo", 1)], axis=0)
    normed = jnp.concatenate([normed] + [shift(normed, "x", e) for e in range(1, nx)], axis=1)
    n_half = [normed, shift(normed, "core", 1)]

    up_keep = dot(w[0], cot, ((1,), (1,)))
    up_send = dot(w[1], cot, ((1,), (1,))).astype(BF16)
    up = (up_keep + shift(up_send, "core", 1).astype(F32)).astype(BF16)
    up = up.reshape(nzl * feat, nx, tok)
    up = sum_f32([up[:, 0]] + [shift(up[:, e], "x", -e) for e in range(1, nx)])
    up = (up[:feat] + shift(up[feat:].astype(BF16), "z_lo", 1).astype(F32)).astype(BF16)
    after = slot + (got[0, 0, 0].astype(F32) * 0.0).astype(jnp.int32)
    place_back = (jnp.arange(slots, dtype=jnp.int32)[:, None] == after[None, :]).astype(BF16)
    back = dot(place_back, up, ((1,), (1,))).astype(BF16).reshape(n_section, block_slots, feat)
    back = exchange(back, SECTION).reshape(nb, nf, n_seq, CAP, feat).transpose(2, 1, 0, 3, 4)
    back = exchange(back.reshape(n_seq, nf * nb * CAP, feat), SEQ)
    back = back.reshape(ny, nzh, nf, nb * CAP, feat).transpose(0, 3, 2, 1, 4)
    upstream = back.reshape(n_seq * CAP, model_width).astype(F32)
    scaled = upstream * gain_full
    row_grads = (
        inv_rms * (scaled - unit_rows * jnp.mean(scaled * unit_rows, axis=-1, keepdims=True))
    ).astype(BF16)
    table_grad = dot(pick_matrix, row_grads, ((1,), (0,))).astype(BF16)

    proj = sum(dot(n, w[c], ((0,), (0,))) for c, n in enumerate(n_half))
    proj = proj.astype(BF16).reshape(nx, tok, cols)
    proj = [pick(proj, (ix - ih - d) % nx) for d in range(nzh)]
    projected = sum_f32([proj[0]] + [shift(proj[d], "z_hi", d) for d in range(1, nzh)]).astype(BF16)

    grad = jnp.concatenate([dot(n, cot, ((1,), (0,))).astype(BF16) for n in n_half], axis=0)
    grad = grad.reshape(nf, feat, cols)

    def slice_for(d):
        f = (iy + d) % ny
        return pick(grad, (ic ^ (f % nc)) * nzl + (iz ^ (f // nc)))
    weight_grad = sum_f32(
        [slice_for(0)] + [shift(slice_for(d), "y", d) for d in range(1, ny)]
    ).astype(BF16)
    return projected, table_grad, weight_grad


def solution(mesh):
    devices = mesh.devices.reshape(4, 2, 2, 4, 4)
    fine = Mesh(devices, SECTION + SEQ)
    in_specs = (
        P(SECTION + SEQ, None),
        P(SEQ, None),
        P(SEQ),
        P(),
        P(SEQ, SECTION),
        P(SEQ, SECTION),
    )
    out_specs = (P(SEQ, SECTION), P(SECTION + SEQ, None), P(SEQ, SECTION))
    return jax.shard_map(
        per_device, mesh=fine, in_specs=in_specs, out_specs=out_specs, check_vma=False
    )
```

```python
import functools

import jax
import jax.numpy as jnp
from jax import lax
from jax.experimental import pallas as pl
from jax.experimental.pallas import tpu as pltpu
from jax.sharding import Mesh, PartitionSpec as P

EPS = 1e-06
SECTION = ("x", "z_lo", "core")
SEQ = ("y", "z_hi")
CAP = 2
BF16 = jnp.bfloat16
F32 = jnp.float32
I32 = jnp.int32
VMEM_LIMIT = 40 * 1024 * 1024
VMEM_WHOLE = 60 * 1024 * 1024

NX, NZL, NC, NY, NZH = 4, 2, 2, 4, 4
N_SECTION, N_SEQ = NX * NZL * NC, NY * NZH
NB, NF = NX, NZL * NC
BLOCK_SLOTS = N_SEQ * CAP
SLOTS = N_SECTION * BLOCK_SLOTS
GROUP = NB * CAP


def dot(a, b, contract):
    return lax.dot_general(a, b, (contract, ((), ())), preferred_element_type=F32)


def shift(x, axis, by):
    size = lax.axis_size(axis)
    return lax.ppermute(x, axis, [(i, (i + by) % size) for i in range(size)])


def swap(x, axis, k):
    return lax.ppermute(x, axis, [(i, i ^ k) for i in range(lax.axis_size(axis))])


def exchange(x, axes):
    return lax.all_to_all(x, axes, split_axis=0, concat_axis=0, tiled=True)


def call(kernel, out_shape, args, flops, scalars=1, scratch=(), after=(), in_hbm=0):
    specs = [pl.BlockSpec(memory_space=pltpu.SMEM)] * scalars
    specs += [pl.BlockSpec(memory_space=pltpu.VMEM)] * (len(args) - scalars - in_hbm)
    specs += [pl.BlockSpec(memory_space=pltpu.HBM)] * in_hbm
    leaves = jax.tree.leaves(out_shape)
    moved = sum(a.size * a.dtype.itemsize for a in list(args) + leaves)
    if after:
        specs = [pl.BlockSpec(memory_space=pl.ANY)] * len(after) + specs
        args, inner = (*after, *args), kernel

        def kernel(*refs):
            inner(*refs[len(after) :])

    return pl.pallas_call(
        kernel,
        out_shape=out_shape,
        in_specs=specs,
        out_specs=jax.tree.map(lambda _: pl.BlockSpec(memory_space=pltpu.VMEM), out_shape),
        scratch_shapes=scratch,
        compiler_params=pltpu.CompilerParams(
            vmem_limit_bytes=VMEM_WHOLE if in_hbm else VMEM_LIMIT
        ),
        cost_estimate=pl.CostEstimate(flops=flops, bytes_accessed=moved, transcendentals=0),
    )(*args)


def iota(shape, dim):
    return lax.broadcasted_iota(I32, shape, dim)


def rows_kernel(place_ref, ids_ref, gain_ref, table_ref, out_ref, rows_ref, wanted_ref, held, table, embedded, arrived):
    vocab_rows, width = table_ref.shape
    feat = out_ref.shape[-1]
    pieces = arrived.shape[0]
    columns = width // pieces
    copies = [
        pltpu.make_async_copy(
            table_ref.at[:, i * columns : (i + 1) * columns], table.at[i], arrived.at[i]
        )
        for i in range(pieces)
    ]
    for copy in copies:
        copy.start()
    n_rows, tok = N_SEQ * CAP, ids_ref.shape[1]
    which = iota((n_rows, tok), 0)
    ids = jnp.zeros((n_rows, tok), I32)
    for j in range(N_SEQ):
        ids = jnp.where(which // CAP == j, jnp.broadcast_to(ids_ref[j : j + 1, :], ids.shape), ids)
    mine = ids // vocab_rows == place_ref[0]
    token = iota((n_rows, tok), 1)
    first = jnp.min(jnp.where(mine, token, tok), axis=1, keepdims=True)
    last = jnp.max(jnp.where(mine, token, -1), axis=1, keepdims=True)
    second = which[:, :1] % CAP == 1
    chosen = jnp.where(second, last, first)
    row = jnp.sum(jnp.where(token == chosen, ids % vocab_rows, 0), axis=1, keepdims=True)
    there = jnp.logical_and(last >= 0, jnp.logical_or(jnp.logical_not(second), last != first))
    wanted = jnp.where(there, row, -1)
    wanted_ref[...] = jnp.broadcast_to(wanted, wanted_ref.shape)
    chooser = jnp.where(iota((n_rows, vocab_rows), 1) == wanted, 1.0, 0.0).astype(BF16)
    squares = jnp.zeros((n_rows, 1), F32)
    for i, copy in enumerate(copies):
        copy.wait()
        part = dot(chooser, table[i], ((1,), (0,)))
        embedded[:, i * columns : (i + 1) * columns] = part
        squares += jnp.sum(part * part, axis=1, keepdims=True)
    rows_ref[...] = embedded[...].astype(BF16)
    inv_rms = lax.rsqrt(squares / width + EPS)
    normed = (embedded[...] * inv_rms) * gain_ref[...].astype(F32)
    for f in range(NF):
        for z in range(NZH):
            start = (f * NZH + z) * feat
            low = start // 128 * 128
            high = min(-(-(start + feat) // 128) * 128, width)
            part = normed[:, low:high]
            if start != low:
                part = pltpu.roll(part, (high - low) - (start - low), 1)
            for y in range(NY):
                held[y * NZH + z, f * GROUP : (f + 1) * GROUP, :] = part[
                    y * GROUP : (y + 1) * GROUP, :feat
                ]
    out_ref[...] = held[...].astype(BF16)


def upstream_kernel(place_ref, *refs):
    cots, ws, (keep_ref, send_ref) = refs[:2], refs[2 : 2 + NY], refs[2 + NY :]
    ih, iy, core = place_ref[0], place_ref[1], place_ref[2]
    half = cots[0].shape[1] // NC

    def tokens(c):
        at = pl.ds(pl.multiple_of(c * half, half), half)
        return jnp.concatenate([cots[k // 2][k % 2, at, :] for k in range(NZH)], axis=0)

    keep, send = tokens(core), tokens(1 - core)
    for d, w in enumerate(ws):
        f = (iy - d + NY) % NY
        for tokens_of, ref in ((send, send_ref), (keep, keep_ref)):
            part = dot(tokens_of, w[...], ((1,), (1,))).astype(ref.dtype)
            for k in range(NZH):
                ref[f, ih ^ k] = part[k * half : (k + 1) * half]


def to_section_kernel(got_ref, keep_ref, recv_ref, out_ref):
    feat = got_ref.shape[-1]
    to, of = iota((SLOTS, SLOTS), 0), iota((SLOTS, SLOTS), 1)
    b, f, v, r = to // 128, to // 32 % 4, to // 2 % 16, to % 2
    order = jnp.where(of == v * 32 + f * 8 + b * 2 + r, 1.0, 0.0).astype(BF16)
    rows = dot(order, got_ref[...].reshape(SLOTS, feat), ((1,), (0,))).astype(BF16)
    out_ref[:, :BLOCK_SLOTS, :] = rows.reshape(N_SECTION, BLOCK_SLOTS, feat)
    for b in range(NB):
        for f in range(NF):
            total = keep_ref[f, b] + recv_ref[f, b].astype(F32)
            out_ref[b * NF + f, BLOCK_SLOTS:, :] = total.astype(BF16)


def at_block_kernel(ids_ref, both_ref, out_ref, *, vocab_rows):
    feat = both_ref.shape[-1]
    tok = ids_ref.shape[1]
    half = tok // NC
    up = []
    for c in range(NC):
        total = both_ref[c, BLOCK_SLOTS:, :].astype(F32)
        for i in range(1, NX * NZL):
            total += both_ref[i * NC + c, BLOCK_SLOTS:, :].astype(F32)
        up.append(total)
    up = jnp.concatenate(up, axis=0).astype(BF16)
    shard_row = jnp.broadcast_to(ids_ref[...] // vocab_rows, (tok, tok))
    down, along = iota((tok, tok), 0), iota((tok, tok), 1)
    shard_col = jnp.sum(jnp.where(down == along, shard_row, 0), axis=1, keepdims=True)
    same = shard_row == shard_col
    rank_col = jnp.sum(jnp.where(jnp.logical_and(same, along < down), 1, 0), axis=1, keepdims=True)
    rank_row = jnp.sum(jnp.where(jnp.logical_and(same, down < along), 1, 0), axis=0, keepdims=True)
    slot_col = shard_col * CAP + rank_col
    slot_row = ids_ref[...] // vocab_rows * CAP + rank_row
    place = jnp.where(iota((tok, SLOTS), 1) == slot_col, 1.0, 0.0).astype(BF16)
    place_back = jnp.where(iota((SLOTS, tok), 0) == slot_row, 1.0, 0.0).astype(BF16)
    got = both_ref[:, :BLOCK_SLOTS, :].reshape(SLOTS, feat)
    normed = dot(place, got, ((1,), (0,))).astype(BF16)
    back = dot(place_back, up, ((1,), (0,))).astype(BF16)
    out_ref[:, :BLOCK_SLOTS, :] = back.reshape(N_SECTION, BLOCK_SLOTS, feat)
    for s in range(N_SECTION):
        c = s % NC
        out_ref[s, BLOCK_SLOTS:, :] = normed[c * half : (c + 1) * half]


def to_seq_kernel(both_ref, out_ref):
    feat = both_ref.shape[-1]
    to, of = iota((SLOTS, SLOTS), 0), iota((SLOTS, SLOTS), 1)
    v, f, b, r = to // 32, to // 8 % 4, to // 2 % 4, to % 2
    order = jnp.where(of == b * 128 + f * 32 + v * 2 + r, 1.0, 0.0).astype(BF16)
    rows = both_ref[:, :BLOCK_SLOTS, :].reshape(SLOTS, feat)
    rows = dot(order, rows, ((1,), (0,))).astype(BF16)
    out_ref[...] = rows.reshape(N_SEQ, BLOCK_SLOTS, feat)


def products_kernel(place_ref, own_ref, other_ref, *refs):
    sources, refs = refs[: 2 + NY], refs[2 + NY :]
    projs, grads = refs[:NZH], refs[NZH : NZH + NY]
    cots, ws, arrived = refs[NZH + NY :]
    targets = [cots.at[:2], cots.at[2:]] + [ws.at[d] for d in range(NY)]
    copies = [
        pltpu.make_async_copy(source, target, arrived.at[i])
        for i, (source, target) in enumerate(zip(sources, targets))
    ]
    for copy in copies:
        copy.start()
    ih, iy, core = place_ref[0], place_ref[1], place_ref[2]
    tok = cots.shape[1]
    half = tok // NC
    at = [pl.ds(pl.multiple_of(c * half, half), half) for c in (core, 1 - core)]
    blocks = [(ih + d) % NZH for d in range(NZH)]
    copies[0].wait()
    copies[1].wait()
    cot = jnp.concatenate([cots[b ^ ih, a, :] for b in blocks for a in at], axis=0)
    proj = None
    for d in range(NY):
        f = (iy + d) % NY
        parts = []
        for b in blocks:
            parts += [ref[b * NF + f, BLOCK_SLOTS:, :] for ref in (own_ref, other_ref)]
        normed = jnp.concatenate(parts, axis=0)
        grads[d][...] = dot(normed, cot, ((0,), (0,))).astype(BF16)
        copies[2 + -d % NY].wait()
        term = dot(normed, ws[-d % NY], ((1,), (0,)))
        proj = term if proj is None else proj + term
    for d in range(NZH):
        for c, a in enumerate(at):
            first = (d * NC + c) * half
            projs[d][a, :] = proj[first : first + half].astype(BF16)


def table_kernel(back_ref, rows_ref, gain_ref, wanted_ref, *refs):
    out_ref, gathered, padded, grads = refs[-4:]
    feat = back_ref.shape[-1]
    n_rows, width = rows_ref.shape
    step, columns = pl.program_id(0), out_ref.shape[1]

    @pl.when(step == 0)
    def _():
        gathered[...] = jnp.zeros_like(gathered)
        padded[...] = jnp.zeros_like(padded)
        for y in range(NY):
            for z in range(NZH):
                part = back_ref[y * NZH + z].astype(F32)
                for f in range(NF):
                    padded[f * NZH + z, y * GROUP : (y + 1) * GROUP, :feat] = part[
                        f * GROUP : (f + 1) * GROUP
                    ]
        for i in range(NF * NZH):
            start = i * feat
            low = start // 128 * 128
            high = min(-(-(start + feat) // 128) * 128, width)
            part = padded[i, :, : high - low]
            if start != low:
                part = pltpu.roll(part, start - low, 1)
            gathered[:, low:high] += part
        embedded = rows_ref[...].astype(F32)
        inv_rms = lax.rsqrt(jnp.mean(embedded * embedded, axis=1, keepdims=True) + EPS)
        unit_rows = embedded * inv_rms
        scaled = gathered[...] * gain_ref[...].astype(F32)
        inner = jnp.mean(scaled * unit_rows, axis=1, keepdims=True)
        result = (inv_rms * (scaled - unit_rows * inner)).astype(BF16)
        for i in range(width // columns):
            grads[i] = result[:, i * columns : (i + 1) * columns]

    chooser = jnp.where(iota((n_rows, out_ref.shape[0]), 1) == wanted_ref[:, :1], 1.0, 0.0)
    out_ref[...] = dot(chooser.astype(BF16), grads[step], ((0,), (0,))).astype(BF16)


def table_call(back, rows, gain, wanted, vocab_rows, after):
    n_rows, width = rows.shape
    feat = back.shape[-1]
    steps = 6
    columns = width // steps
    args = (back, rows, gain, wanted)
    return pl.pallas_call(
        table_kernel,
        grid=(steps,),
        out_shape=jax.ShapeDtypeStruct((vocab_rows, width), BF16),
        in_specs=[pl.BlockSpec(a.shape, lambda i, n=a.ndim: (0,) * n) for a in args]
        + [pl.BlockSpec(memory_space=pl.ANY)] * len(after),
        out_specs=pl.BlockSpec((vocab_rows, columns), lambda i: (0, i)),
        scratch_shapes=[
            pltpu.VMEM((n_rows, width), F32),
            pltpu.VMEM((NF * NZH, n_rows, -(-feat // 128) * 128 + 128), F32),
            pltpu.VMEM((steps, n_rows, columns), BF16),
        ],
        compiler_params=pltpu.CompilerParams(vmem_limit_bytes=VMEM_LIMIT),
        cost_estimate=pl.CostEstimate(
            flops=2 * vocab_rows * n_rows * width, bytes_accessed=2 * vocab_rows * width,
            transcendentals=0,
        ),
    )(*args, *after)


def sum_f32(parts):
    total = parts[0].astype(F32)
    for part in parts[1:]:
        total = total + part.astype(F32)
    return total


def per_device(embed_table, vocab_shard, shard_row, norm_gain, weight, cotangent):
    vocab_rows, model_width = embed_table.shape
    tok = shard_row.shape[0]
    feat, cols = weight.shape
    half = tok // NC
    section, seq = lax.axis_index(SECTION), lax.axis_index(SEQ)
    ix, iz, ic, iy, ih = (lax.axis_index(a) for a in SECTION + SEQ)
    where = jnp.stack([ih, iy, ic]).astype(I32)
    shape = jax.ShapeDtypeStruct

    ids = vocab_shard[:, 0] * vocab_rows + shard_row
    all_ids = exchange(jnp.broadcast_to(ids[None], (N_SEQ, tok)), SEQ)

    ws = [shift(weight, "y", d) for d in range(1, NY)]
    near = swap(cotangent, "z_hi", 1)
    gain = norm_gain.reshape(1, -1)
    all_ids, gain, near, *ws = lax.optimization_barrier((all_ids, gain, near, *ws))
    ws = [weight, *ws]
    near = jnp.stack([cotangent, near])
    cots = [near, swap(near, "z_hi", 2)]

    shard = (section * N_SEQ + seq).astype(I32).reshape(1)
    out_rows, rows, wanted = call(
        rows_kernel,
        (
            shape((N_SEQ, NF * GROUP, feat), BF16),
            shape((N_SEQ * CAP, model_width), BF16),
            shape((N_SEQ * CAP, 128), I32),
        ),
        (shard, all_ids, gain, embed_table),
        flops=2 * N_SEQ * CAP * vocab_rows * model_width,
        in_hbm=1,
        scratch=[
            pltpu.VMEM((N_SEQ, NF * GROUP, feat), F32),
            pltpu.VMEM((6, vocab_rows, model_width // 6), BF16),
            pltpu.VMEM((N_SEQ * CAP, model_width), F32),
            pltpu.SemaphoreType.DMA((6,)),
        ],
    )
    got = exchange(out_rows, SEQ)

    keep, send = call(
        upstream_kernel,
        (shape((NF, NB, half, feat), F32), shape((NF, NB, half, feat), BF16)),
        (where, *cots, *ws),
        flops=2 * NB * tok * NF * feat * cols,
        after=(wanted,),
    )
    recv = jnp.concatenate([swap(send[i : i + 1], "core", 1) for i in range(NF)], axis=0)

    width = BLOCK_SLOTS + half
    both = call(
        to_section_kernel, shape((N_SECTION, width, feat), BF16), (got, keep, recv),
        flops=2 * SLOTS * SLOTS * feat, scalars=0,
    )
    both = exchange(both, SECTION)
    block_ids = lax.dynamic_slice_in_dim(all_ids, iy * NZH + ix, 1, 0)
    both = call(
        functools.partial(at_block_kernel, vocab_rows=vocab_rows),
        shape((N_SECTION, width, feat), BF16), (block_ids, both),
        flops=4 * tok * SLOTS * feat, scalars=0,
    )
    both = exchange(both, SECTION)
    back = call(
        to_seq_kernel, shape((N_SEQ, BLOCK_SLOTS, feat), BF16), (both,),
        flops=2 * SLOTS * SLOTS * feat, scalars=0,
    )
    back = exchange(back, SEQ)

    products = call(
        products_kernel,
        (shape((tok, cols), BF16),) * NZH + (shape((feat, cols), BF16),) * NY,
        (where, both, swap(both, "core", 1), *cots, *ws),
        flops=4 * NB * tok * NF * feat * cols,
        in_hbm=2 + NY,
        scratch=[
            pltpu.VMEM((NZH, tok, cols), BF16),
            pltpu.VMEM((NY, feat, cols), BF16),
            pltpu.SemaphoreType.DMA((2 + NY,)),
        ],
    )
    proj, grad = products[:NZH], products[NZH:]
    grad_parts = [shift(grad[d], "y", d) for d in range(1, NY)]
    proj_parts = [shift(proj[d], "z_hi", d) for d in range(1, NZH)]
    weight_grad = sum_f32([grad[0], *grad_parts]).astype(BF16)
    projected = sum_f32([proj[0], *proj_parts]).astype(BF16)

    table_grad = table_call(back, rows, gain, wanted, vocab_rows, after=proj_parts)
    return projected, table_grad, weight_grad


def solution(mesh):
    fine = Mesh(mesh.devices.reshape(NX, NZL, NC, NY, NZH), SECTION + SEQ)
    in_specs = (
        P(SECTION + SEQ, None),
        P(SEQ, None),
        P(SEQ),
        P(),
        P(SEQ, SECTION),
        P(SEQ, SECTION),
    )
    out_specs = (P(SEQ, SECTION), P(SECTION + SEQ, None), P(SEQ, SECTION))
    return jax.shard_map(
        per_device, mesh=fine, in_specs=in_specs, out_specs=out_specs, check_vma=False
    )
```

```python
import functools

import jax
import jax.numpy as jnp
from jax import lax
from jax.experimental import pallas as pl
from jax.experimental.pallas import tpu as pltpu
from jax.sharding import Mesh, PartitionSpec as P

EPS = 1e-06
SECTION = ("x", "z_lo", "core")
SEQ = ("y", "z_hi")
CAP = 2
BF16 = jnp.bfloat16
F32 = jnp.float32
I32 = jnp.int32
VMEM_LIMIT = 40 * 1024 * 1024
VMEM_WHOLE = 60 * 1024 * 1024

NX, NZL, NC, NY, NZH = 4, 2, 2, 4, 4
N_SECTION, N_SEQ = NX * NZL * NC, NY * NZH
NB, NF = NX, NZL * NC
BLOCK_SLOTS = N_SEQ * CAP
SLOTS = N_SECTION * BLOCK_SLOTS
GROUP = NB * CAP


def dot(a, b, contract):
    return lax.dot_general(a, b, (contract, ((), ())), preferred_element_type=F32)


def shift(x, axis, by):
    size = lax.axis_size(axis)
    return lax.ppermute(x, axis, [(i, (i + by) % size) for i in range(size)])


def swap(x, axis, k):
    return lax.ppermute(x, axis, [(i, i ^ k) for i in range(lax.axis_size(axis))])


def exchange(x, axes):
    return lax.all_to_all(x, axes, split_axis=0, concat_axis=0, tiled=True)


def call(kernel, out_shape, args, flops, scalars=1, scratch=(), after=(), in_hbm=0, limit=None):
    specs = [pl.BlockSpec(memory_space=pltpu.SMEM)] * scalars
    specs += [pl.BlockSpec(memory_space=pltpu.VMEM)] * (len(args) - scalars - in_hbm)
    specs += [pl.BlockSpec(memory_space=pltpu.HBM)] * in_hbm
    leaves = jax.tree.leaves(out_shape)
    moved = sum(a.size * a.dtype.itemsize for a in list(args) + leaves)
    if after:
        specs = [pl.BlockSpec(memory_space=pl.ANY)] * len(after) + specs
        args, inner = (*after, *args), kernel

        def kernel(*refs):
            inner(*refs[len(after) :])

    return pl.pallas_call(
        kernel,
        out_shape=out_shape,
        in_specs=specs,
        out_specs=jax.tree.map(lambda _: pl.BlockSpec(memory_space=pltpu.VMEM), out_shape),
        scratch_shapes=scratch,
        compiler_params=pltpu.CompilerParams(
            vmem_limit_bytes=limit or (VMEM_WHOLE if in_hbm else VMEM_LIMIT)
        ),
        cost_estimate=pl.CostEstimate(flops=flops, bytes_accessed=moved, transcendentals=0),
    )(*args)


def iota(shape, dim):
    return lax.broadcasted_iota(I32, shape, dim)


def rows_kernel(place_ref, ids_ref, gain_ref, table_ref, out_ref, rows_ref, wanted_ref, held, table, embedded, arrived):
    vocab_rows, width = table_ref.shape
    feat = out_ref.shape[-1]
    pieces = arrived.shape[0]
    columns = width // pieces
    copies = [
        pltpu.make_async_copy(
            table_ref.at[:, i * columns : (i + 1) * columns], table.at[i], arrived.at[i]
        )
        for i in range(pieces)
    ]
    for copy in copies:
        copy.start()
    n_rows, tok = N_SEQ * CAP, ids_ref.shape[1]
    which = iota((n_rows, tok), 0)
    ids = jnp.zeros((n_rows, tok), I32)
    for j in range(N_SEQ):
        ids = jnp.where(which // CAP == j, jnp.broadcast_to(ids_ref[j : j + 1, :], ids.shape), ids)
    ids = ids % (vocab_rows * N_SECTION * N_SEQ)
    mine = ids // vocab_rows == place_ref[0]
    token = iota((n_rows, tok), 1)
    first = jnp.min(jnp.where(mine, token, tok), axis=1, keepdims=True)
    last = jnp.max(jnp.where(mine, token, -1), axis=1, keepdims=True)
    second = which[:, :1] % CAP == 1
    chosen = jnp.where(second, last, first)
    row = jnp.sum(jnp.where(token == chosen, ids % vocab_rows, 0), axis=1, keepdims=True)
    there = jnp.logical_and(last >= 0, jnp.logical_or(jnp.logical_not(second), last != first))
    wanted = jnp.where(there, row, -1)
    wanted_ref[...] = jnp.broadcast_to(wanted, wanted_ref.shape)
    chooser = jnp.where(iota((n_rows, vocab_rows), 1) == wanted, 1.0, 0.0).astype(BF16)
    squares = jnp.zeros((n_rows, 1), F32)
    for i, copy in enumerate(copies):
        copy.wait()
        part = dot(chooser, table[i], ((1,), (0,)))
        embedded[:, i * columns : (i + 1) * columns] = part
        squares += jnp.sum(part * part, axis=1, keepdims=True)
    rows_ref[...] = embedded[...].astype(BF16)
    inv_rms = lax.rsqrt(squares / width + EPS)
    normed = (embedded[...] * inv_rms) * gain_ref[...].astype(F32)
    for f in range(NF):
        for z in range(NZH):
            start = (f * NZH + z) * feat
            low = start // 128 * 128
            high = min(-(-(start + feat) // 128) * 128, width)
            part = normed[:, low:high]
            if start != low:
                part = pltpu.roll(part, (high - low) - (start - low), 1)
            for y in range(NY):
                held[y * NZH + z, f * GROUP : (f + 1) * GROUP, :] = part[
                    y * GROUP : (y + 1) * GROUP, :feat
                ]
    out_ref[...] = held[...].astype(BF16)


def upstream_kernel(place_ref, *refs):
    cots, ws, (keep_ref, send_ref) = refs[:2], refs[2 : 2 + NY], refs[2 + NY :]
    ih, iy, core = place_ref[0], place_ref[1], place_ref[2]
    half = cots[0].shape[1] // NC

    def tokens(c):
        at = pl.ds(pl.multiple_of(c * half, half), half)
        return jnp.concatenate([cots[k // 2][k % 2, at, :] for k in range(NZH)], axis=0)

    keep, send = tokens(core), tokens(1 - core)
    for d, w in enumerate(ws):
        f = (iy - d + NY) % NY
        for tokens_of, ref in ((send, send_ref), (keep, keep_ref)):
            part = dot(tokens_of, w[...], ((1,), (1,))).astype(ref.dtype)
            for k in range(NZH):
                ref[f, ih ^ k] = part[k * half : (k + 1) * half]


def to_section_kernel(got_ref, keep_ref, recv_ref, out_ref):
    feat = got_ref.shape[-1]
    to, of = iota((SLOTS, SLOTS), 0), iota((SLOTS, SLOTS), 1)
    b, f, v, r = to // 128, to // 32 % 4, to // 2 % 16, to % 2
    order = jnp.where(of == v * 32 + f * 8 + b * 2 + r, 1.0, 0.0).astype(BF16)
    rows = dot(order, got_ref[...].reshape(SLOTS, feat), ((1,), (0,))).astype(BF16)
    out_ref[:, :BLOCK_SLOTS, :] = rows.reshape(N_SECTION, BLOCK_SLOTS, feat)
    for b in range(NB):
        for f in range(NF):
            total = keep_ref[f, b] + recv_ref[f, b].astype(F32)
            out_ref[b * NF + f, BLOCK_SLOTS:, :] = total.astype(BF16)


def at_block_kernel(ids_ref, both_ref, out_ref, *, vocab_rows):
    feat = both_ref.shape[-1]
    tok = ids_ref.shape[1]
    half = tok // NC
    up = []
    for c in range(NC):
        total = both_ref[c, BLOCK_SLOTS:, :].astype(F32)
        for i in range(1, NX * NZL):
            total += both_ref[i * NC + c, BLOCK_SLOTS:, :].astype(F32)
        up.append(total)
    up = jnp.concatenate(up, axis=0).astype(BF16)
    shard_row = jnp.broadcast_to(ids_ref[...] // vocab_rows, (tok, tok))
    down, along = iota((tok, tok), 0), iota((tok, tok), 1)
    shard_col = jnp.sum(jnp.where(down == along, shard_row, 0), axis=1, keepdims=True)
    same = shard_row == shard_col
    rank_col = jnp.sum(jnp.where(jnp.logical_and(same, along < down), 1, 0), axis=1, keepdims=True)
    rank_row = jnp.sum(jnp.where(jnp.logical_and(same, down < along), 1, 0), axis=0, keepdims=True)
    slot_col = shard_col * CAP + rank_col
    slot_row = ids_ref[...] // vocab_rows * CAP + rank_row
    place = jnp.where(iota((tok, SLOTS), 1) == slot_col, 1.0, 0.0).astype(BF16)
    place_back = jnp.where(iota((SLOTS, tok), 0) == slot_row, 1.0, 0.0).astype(BF16)
    got = both_ref[:, :BLOCK_SLOTS, :].reshape(SLOTS, feat)
    normed = dot(place, got, ((1,), (0,))).astype(BF16)
    back = dot(place_back, up, ((1,), (0,))).astype(BF16)
    out_ref[:, :BLOCK_SLOTS, :] = back.reshape(N_SECTION, BLOCK_SLOTS, feat)
    for s in range(N_SECTION):
        c = s % NC
        out_ref[s, BLOCK_SLOTS:, :] = normed[c * half : (c + 1) * half]


def to_seq_kernel(both_ref, out_ref):
    feat = both_ref.shape[-1]
    to, of = iota((SLOTS, SLOTS), 0), iota((SLOTS, SLOTS), 1)
    v, f, b, r = to // 32, to // 8 % 4, to // 2 % 4, to % 2
    order = jnp.where(of == b * 128 + f * 32 + v * 2 + r, 1.0, 0.0).astype(BF16)
    rows = both_ref[:, :BLOCK_SLOTS, :].reshape(SLOTS, feat)
    rows = dot(order, rows, ((1,), (0,))).astype(BF16)
    out_ref[...] = rows.reshape(N_SEQ, BLOCK_SLOTS, feat)


def products_kernel(place_ref, own_ref, other_ref, *refs):
    sources, refs = refs[: 2 + NY], refs[2 + NY :]
    projs, grads = refs[:NZH], refs[NZH : NZH + NY]
    cots, ws, arrived = refs[NZH + NY :]
    targets = [cots.at[:2], cots.at[2:]] + [ws.at[d] for d in range(NY)]
    copies = [
        pltpu.make_async_copy(source, target, arrived.at[i])
        for i, (source, target) in enumerate(zip(sources, targets))
    ]
    for copy in copies:
        copy.start()
    ih, iy, core = place_ref[0], place_ref[1], place_ref[2]
    tok = cots.shape[1]
    half = tok // NC
    at = [pl.ds(pl.multiple_of(c * half, half), half) for c in (core, 1 - core)]
    blocks = [(ih + d) % NZH for d in range(NZH)]
    copies[0].wait()
    copies[1].wait()
    cot = jnp.concatenate([cots[b ^ ih, a, :] for b in blocks for a in at], axis=0)
    proj = None
    for d in range(NY):
        f = (iy + d) % NY
        parts = []
        for b in blocks:
            parts += [ref[b * NF + f, BLOCK_SLOTS:, :] for ref in (own_ref, other_ref)]
        normed = jnp.concatenate(parts, axis=0)
        grads[d][...] = dot(normed, cot, ((0,), (0,))).astype(BF16)
        copies[2 + -d % NY].wait()
        term = dot(normed, ws[-d % NY], ((1,), (0,)))
        proj = term if proj is None else proj + term
    for d in range(NZH):
        for c, a in enumerate(at):
            first = (d * NC + c) * half
            projs[d][a, :] = proj[first : first + half].astype(BF16)


def table_kernel(back_ref, rows_ref, gain_ref, wanted_ref, *refs):
    out_ref, gathered, padded, grads = refs[-4:]
    feat = back_ref.shape[-1]
    n_rows, width = rows_ref.shape
    step, columns = pl.program_id(0), out_ref.shape[1]

    @pl.when(step == 0)
    def _():
        gathered[...] = jnp.zeros_like(gathered)
        padded[...] = jnp.zeros_like(padded)
        for y in range(NY):
            for z in range(NZH):
                part = back_ref[y * NZH + z].astype(F32)
                for f in range(NF):
                    padded[f * NZH + z, y * GROUP : (y + 1) * GROUP, :feat] = part[
                        f * GROUP : (f + 1) * GROUP
                    ]
        for i in range(NF * NZH):
            start = i * feat
            low = start // 128 * 128
            high = min(-(-(start + feat) // 128) * 128, width)
            part = padded[i, :, : high - low]
            if start != low:
                part = pltpu.roll(part, start - low, 1)
            gathered[:, low:high] += part
        embedded = rows_ref[...].astype(F32)
        inv_rms = lax.rsqrt(jnp.mean(embedded * embedded, axis=1, keepdims=True) + EPS)
        unit_rows = embedded * inv_rms
        scaled = gathered[...] * gain_ref[...].astype(F32)
        inner = jnp.mean(scaled * unit_rows, axis=1, keepdims=True)
        result = (inv_rms * (scaled - unit_rows * inner)).astype(BF16)
        for i in range(width // columns):
            grads[i] = result[:, i * columns : (i + 1) * columns]

    chooser = jnp.where(iota((n_rows, out_ref.shape[0]), 1) == wanted_ref[:, :1], 1.0, 0.0)
    out_ref[...] = dot(chooser.astype(BF16), grads[step], ((0,), (0,))).astype(BF16)


def table_call(back, rows, gain, wanted, vocab_rows, after):
    n_rows, width = rows.shape
    feat = back.shape[-1]
    steps = 6
    columns = width // steps
    args = (back, rows, gain, wanted)
    return pl.pallas_call(
        table_kernel,
        grid=(steps,),
        out_shape=jax.ShapeDtypeStruct((vocab_rows, width), BF16),
        in_specs=[pl.BlockSpec(a.shape, lambda i, n=a.ndim: (0,) * n) for a in args]
        + [pl.BlockSpec(memory_space=pl.ANY)] * len(after),
        out_specs=pl.BlockSpec((vocab_rows, columns), lambda i: (0, i)),
        scratch_shapes=[
            pltpu.VMEM((n_rows, width), F32),
            pltpu.VMEM((NF * NZH, n_rows, -(-feat // 128) * 128 + 128), F32),
            pltpu.VMEM((steps, n_rows, columns), BF16),
        ],
        compiler_params=pltpu.CompilerParams(vmem_limit_bytes=VMEM_LIMIT),
        cost_estimate=pl.CostEstimate(
            flops=2 * vocab_rows * n_rows * width, bytes_accessed=2 * vocab_rows * width,
            transcendentals=0,
        ),
    )(*args, *after)


def sum_f32(parts):
    total = parts[0].astype(F32)
    for part in parts[1:]:
        total = total + part.astype(F32)
    return total


def per_device(embed_table, vocab_shard, shard_row, norm_gain, weight, cotangent):
    vocab_rows, model_width = embed_table.shape
    tok = shard_row.shape[0]
    feat, cols = weight.shape
    half = tok // NC
    section, seq = lax.axis_index(SECTION), lax.axis_index(SEQ)
    ix, iz, ic, iy, ih = (lax.axis_index(a) for a in SECTION + SEQ)
    where = jnp.stack([ih, iy, ic]).astype(I32)
    shape = jax.ShapeDtypeStruct

    ids = vocab_shard[:, 0] * vocab_rows + shard_row
    vocab = vocab_rows * N_SECTION * N_SEQ
    all_ids = exchange(ids[None] + vocab * jnp.arange(N_SEQ, dtype=I32)[:, None], SEQ)

    ws = [shift(weight, "y", d) for d in range(1, NY)]
    near = swap(cotangent, "z_hi", 1)
    gain = norm_gain.reshape(1, -1)
    all_ids, gain, near, *ws = lax.optimization_barrier((all_ids, gain, near, *ws))
    ws = [weight, *ws]
    near = jnp.stack([cotangent, near])
    cots = [near, swap(near, "z_hi", 2)]

    shard = (section * N_SEQ + seq).astype(I32).reshape(1)
    out_rows, rows, wanted = call(
        rows_kernel,
        (
            shape((N_SEQ, NF * GROUP, feat), BF16),
            shape((N_SEQ * CAP, model_width), BF16),
            shape((N_SEQ * CAP, 128), I32),
        ),
        (shard, all_ids, gain, embed_table),
        flops=2 * N_SEQ * CAP * vocab_rows * model_width,
        in_hbm=1,
        limit=50 * 1024 * 1024,
        scratch=[
            pltpu.VMEM((N_SEQ, NF * GROUP, feat), F32),
            pltpu.VMEM((6, vocab_rows, model_width // 6), BF16),
            pltpu.VMEM((N_SEQ * CAP, model_width), F32),
            pltpu.SemaphoreType.DMA((6,)),
        ],
    )
    got = exchange(out_rows, SEQ)

    keep, send = call(
        upstream_kernel,
        (shape((NF, NB, half, feat), F32), shape((NF, NB, half, feat), BF16)),
        (where, *cots, *ws),
        flops=2 * NB * tok * NF * feat * cols,
        after=(wanted,),
    )
    recv = jnp.concatenate([swap(send[i : i + 1], "core", 1) for i in range(NF)], axis=0)

    width = BLOCK_SLOTS + half
    both = call(
        to_section_kernel, shape((N_SECTION, width, feat), BF16), (got, keep, recv),
        flops=2 * SLOTS * SLOTS * feat, scalars=0,
    )
    both = exchange(both, SECTION)
    block_ids = lax.dynamic_slice_in_dim(all_ids, iy * NZH + ix, 1, 0) % vocab
    both = call(
        functools.partial(at_block_kernel, vocab_rows=vocab_rows),
        shape((N_SECTION, width, feat), BF16), (block_ids, both),
        flops=4 * tok * SLOTS * feat, scalars=0,
    )
    both = exchange(both, SECTION)
    cut = call(
        to_seq_kernel, shape((N_SEQ, BLOCK_SLOTS, feat), BF16), (both,),
        flops=2 * SLOTS * SLOTS * feat, scalars=0,
    )
    back = exchange(cut, SEQ)

    products = call(
        products_kernel,
        (shape((tok, cols), BF16),) * NZH + (shape((feat, cols), BF16),) * NY,
        (where, both, swap(both, "core", 1), *cots, *ws),
        flops=4 * NB * tok * NF * feat * cols,
        in_hbm=2 + NY,
        after=(cut,),
        scratch=[
            pltpu.VMEM((NZH, tok, cols), BF16),
            pltpu.VMEM((NY, feat, cols), BF16),
            pltpu.SemaphoreType.DMA((2 + NY,)),
        ],
    )
    proj, grad = products[:NZH], products[NZH:]
    grad_parts = [shift(grad[d], "y", d) for d in range(1, NY)]
    proj_parts = [shift(proj[d], "z_hi", d) for d in range(1, NZH)]
    weight_grad = sum_f32([grad[0], *grad_parts]).astype(BF16)
    projected = sum_f32([proj[0], *proj_parts]).astype(BF16)

    table_grad = table_call(back, rows, gain, wanted, vocab_rows, after=proj_parts[:1])
    return projected, table_grad, weight_grad


def solution(mesh):
    fine = Mesh(mesh.devices.reshape(NX, NZL, NC, NY, NZH), SECTION + SEQ)
    in_specs = (
        P(SECTION + SEQ, None),
        P(SEQ, None),
        P(SEQ),
        P(),
        P(SEQ, SECTION),
        P(SEQ, SECTION),
    )
    out_specs = (P(SEQ, SECTION), P(SECTION + SEQ, None), P(SEQ, SECTION))
    return jax.shard_map(
        per_device, mesh=fine, in_specs=in_specs, out_specs=out_specs, check_vma=False
    )
```
